128 devices in a mesh: seq: 32 (over x, y, core), head: 4 (over z).
Axes of the slice: x: 4, y: 4, z: 4, core: 2. Of those that a mesh axis runs over, the one named last changes fastest.
Arguments:
- tokens: bfloat16 [8192, 2048], P('seq'), may hold values from -6 to 6
- w_query: bfloat16 [2048, 2048], P(None, 'head'), may hold values from -0.125 to 0.125
- w_key: bfloat16 [2048, 2048], P(None, 'head'), may hold values from -0.125 to 0.125
- w_value: bfloat16 [2048, 2048], P(None, 'head'), may hold values from -0.125 to 0.125
- w_beta: bfloat16 [2048, 16], P(None, 'head'), may hold values from -0.125 to 0.125
- b_beta: float32 [16], P('head'), may hold values from -6 to 1
- d_out: bfloat16 [8192, 2048], P('seq', 'head'), may hold values from -6 to 6
Outputs:
- d_x: bfloat16 [8192, 2048], P('seq', 'head')
- grad_query: float32 [2048, 2048], P('seq', 'head')
- grad_key: float32 [2048, 2048], P('seq', 'head')
- grad_value: float32 [2048, 2048], P('seq', 'head')
- grad_wbeta: float32 [2048, 16], P('seq', 'head')
- grad_bbeta: float32 [16], P('head')
The draws below stay inside these ranges and needn't reach their ends.
All inputs are finite; a program needn't handle non-finite values.
Results may differ from the reference program's by a relative error of at most 0.012.
Values may be sent and summed in bfloat16 or wider, within the bound.
No kernel may reach another device: no remote copies, remote signals or barrier semaphores. Data moves between devices by JAX's collectives and lax.ppermute only.
A program may use at most 128 MiB of HBM per device.

```python
import jax
import jax.numpy as jnp
from jax import lax

H = 16
DK = 128
D = 2048
SPAN = 64
TOKENS = 8192


def with_spikes(result, key, source, target, parts, factor):
    owner, partner = [(jnp.arange(result.shape[dim]) // (result.shape[dim] // parts)).reshape([-1 if axis == dim else 1 for axis in range(result.ndim)]) for dim in (source, target)]
    chosen = jax.random.permutation(key, parts)[partner]
    strong = (owner == chosen) | (owner == (partner + parts // 2) % parts)
    return jnp.where(strong, factor * result, result)


def levels(own_key, dims, cuts, low, top_value):
    def one(position, blocks):
        draws = jax.random.uniform(jax.random.fold_in(jax.random.fold_in(own_key, 6), position), (blocks,), jnp.float32, low / len(cuts), top_value / len(cuts))
        return jnp.repeat(jnp.exp(draws), dims[position] // blocks).reshape((-1,) + (1,) * (len(dims) - position - 1))

    gain = one(*cuts[0])
    for cut in cuts[1:]:
        gain = gain * one(*cut)
    return gain


def centred(stream_key, extent, width, bound, cuts=(), held_as=jnp.bfloat16):
    values = jax.random.normal(stream_key, extent, jnp.float32) * width
    if len(cuts) > 0:
        values = levels(stream_key, extent, cuts, -0.22, 0.18) * values
    return jnp.clip(values, min=-bound, max=bound).astype(held_as)


def bell_draw_with(stream_key, extent, deviation, limit, cuts, heavy, kind=jnp.bfloat16):
    values = deviation * jax.random.normal(stream_key, extent, jnp.float32)
    if cuts:
        values = values * levels(stream_key, extent, cuts, -0.22, 0.18)
    return jnp.clip(with_spikes(values, jax.random.fold_in(stream_key, 3), *heavy), -limit, limit).astype(kind)


def setup_inputs(seed: int = 0) -> dict:
    key_list = jax.random.split(jax.random.key(seed), 8)
    tokens = bell_draw_with(key_list[0], (TOKENS, D), 1.0, 6.0, ((0, 32),), (0, 1, 32, 2.75))
    w_query = centred(key_list[1], (D, D), D ** -0.5, 0.125, ((1, 4),))
    w_key = centred(key_list[2], (D, D), D ** -0.5, 0.125, ((1, 4),))
    w_value = centred(key_list[3], (D, D), D ** -0.5, 0.125, ((1, 4),))
    w_beta = centred(key_list[4], (D, H), D ** -0.5, 0.125, ((1, 4),))
    b_beta = jnp.clip(-6.0 + 7.0 * jax.random.uniform(key_list[5], (H,), jnp.float32) ** levels(key_list[5], (H,), ((0, 4),), -0.2, 0.2), -6.0, 1.0)
    d_out = centred(key_list[6], (TOKENS, D), 1.0, 6.0, ((0, 32), (1, 4)))
    return {"tokens": tokens, "w_query": w_query, "w_key": w_key, "w_value": w_value, "w_beta": w_beta, "b_beta": b_beta, "d_out": d_out}


highest = lax.Precision.HIGHEST
epsilon = 1e-06

def delta_block(carry_state, query_block, key_block, value_block, beta_block):
    block_len = key_block.shape[1]
    strict_lower = jnp.tril(jnp.ones((block_len, block_len), key_block.dtype), -1)
    with_diagonal = jnp.tril(jnp.ones((block_len, block_len), key_block.dtype))
    weighted = beta_block[..., None] * key_block
    gram_matrix = jnp.einsum('hcd,hed->hce', weighted, key_block, precision=highest)
    system = jnp.eye(block_len, dtype=key_block.dtype) + gram_matrix * strict_lower
    w_block = lax.linalg.triangular_solve(system, weighted, left_side=True, lower=True, unit_diagonal=True)
    u_block = lax.linalg.triangular_solve(system, beta_block[..., None] * value_block, left_side=True, lower=True, unit_diagonal=True)
    updates = u_block - jnp.einsum('hcd,hvd->hcv', w_block, carry_state, precision=highest)
    scores = jnp.einsum('hcd,hed->hce', query_block, key_block, precision=highest) * with_diagonal
    outputs = jnp.einsum('hcd,hvd->hcv', query_block, carry_state, precision=highest)
    outputs = outputs + jnp.einsum('hce,hev->hcv', scores, updates, precision=highest)
    carry_state = carry_state + jnp.einsum('hcv,hcd->hvd', updates, key_block, precision=highest)
    return (carry_state, outputs, w_block)

def arrange(tensor):
    blocks_count = tensor.shape[0] // SPAN
    shaped = tensor.reshape((blocks_count, SPAN) + tensor.shape[1:])
    return jnp.swapaxes(shaped, 1, 2)

def prepare(query_raw, key_raw, value_raw, logits):
    query_norm = query_raw * lax.rsqrt(lax.optimization_barrier(jnp.sum(query_raw * query_raw, -1, keepdims=True)) + epsilon)
    key_norm = key_raw * lax.rsqrt(lax.optimization_barrier(jnp.sum(key_raw * key_raw, -1, keepdims=True)) + epsilon)
    beta_gate = 2.0 * jax.nn.sigmoid(logits)
    return (arrange(query_norm), arrange(key_norm), arrange(value_raw), arrange(beta_gate))

def delta_layer(query_raw, key_raw, value_raw, logits, initial):
    token_count, head_count, head_width = query_raw.shape
    arranged = prepare(query_raw, key_raw, value_raw, logits)

    def advance(carry_state, pieces):
        carry_state, outputs, unused = delta_block(carry_state, pieces[0], pieces[1], pieces[2], pieces[3])
        return (carry_state, outputs)
    last_state, outputs = lax.scan(jax.checkpoint(advance), initial, arranged)
    outputs = jnp.swapaxes(outputs, 1, 2).reshape(token_count, head_count, head_width)
    return (outputs, last_state)

def reference(tokens, w_query, w_key, w_value, w_beta, b_beta, d_out):
    token_count = tokens.shape[0]
    query_raw = jnp.dot(tokens.astype(jnp.float32), w_query.astype(jnp.float32), preferred_element_type=jnp.float32).reshape(token_count, H, DK)
    key_raw = jnp.dot(tokens.astype(jnp.float32), w_key.astype(jnp.float32), preferred_element_type=jnp.float32).reshape(token_count, H, DK)
    value_raw = jnp.dot(tokens.astype(jnp.float32), w_value.astype(jnp.float32), preferred_element_type=jnp.float32).reshape(token_count, H, DK)
    logits = jnp.dot(tokens.astype(jnp.float32), w_beta.astype(jnp.float32), preferred_element_type=jnp.float32) + b_beta
    initial = jnp.zeros((H, DK, DK), jnp.float32)

    def forward(first_in, second_in, third_in, fourth_in):
        return delta_layer(first_in, second_in, third_in, fourth_in, initial)[0]
    unused, pull_back = jax.vjp(forward, query_raw, key_raw, value_raw, logits)
    cotangent = d_out.astype(jnp.float32).reshape(token_count, H, DK)
    grad_q, grad_k, grad_v, grad_z = pull_back(cotangent)
    query_b = grad_q.reshape(token_count, D).astype(jnp.bfloat16)
    key_b = grad_k.reshape(token_count, D).astype(jnp.bfloat16)
    value_b = grad_v.reshape(token_count, D).astype(jnp.bfloat16)
    logit_b = grad_z.astype(jnp.bfloat16)
    input_grad = jnp.dot(query_b.astype(jnp.float32), w_query.T.astype(jnp.float32), preferred_element_type=jnp.float32)
    input_grad = input_grad + jnp.dot(key_b.astype(jnp.float32), w_key.T.astype(jnp.float32), preferred_element_type=jnp.float32)
    input_grad = input_grad + jnp.dot(value_b.astype(jnp.float32), w_value.T.astype(jnp.float32), preferred_element_type=jnp.float32)
    input_grad = input_grad + jnp.dot(logit_b.astype(jnp.float32), w_beta.T.astype(jnp.float32), preferred_element_type=jnp.float32)
    d_x = input_grad.astype(jnp.bfloat16)
    grad_query = jnp.dot(tokens.T.astype(jnp.float32), query_b.astype(jnp.float32), preferred_element_type=jnp.float32)
    grad_key = jnp.dot(tokens.T.astype(jnp.float32), key_b.astype(jnp.float32), preferred_element_type=jnp.float32)
    grad_value = jnp.dot(tokens.T.astype(jnp.float32), value_b.astype(jnp.float32), preferred_element_type=jnp.float32)
    grad_wbeta = jnp.dot(tokens.T.astype(jnp.float32), logit_b.astype(jnp.float32), preferred_element_type=jnp.float32)
    grad_bbeta = lax.optimization_barrier(jnp.sum(grad_z, 0))
    return (d_x, grad_query, grad_key, grad_value, grad_wbeta, grad_bbeta)
```

```python
import functools

import jax
import jax.numpy as jnp
from jax import lax
from jax.experimental import pallas as pl
from jax.experimental.pallas import tpu as pltpu
from jax.sharding import PartitionSpec as P

EPSILON = 1e-06
WIDTH = 128
ROWS = 256
PAIR = 2 * WIDTH
CHIPS = 16
STRIP = 16
PACK = 3 * PAIR + WIDTH
VMEM = 50 * 2**20
f32 = jnp.float32
bf16 = jnp.bfloat16
STATE = jnp.float32

NN = (((1,), (0,)), ((), ()))
NT = (((1,), (1,)), ((), ()))
TN = (((0,), (0,)), ((), ()))


def split(x):
    high = x.astype(bf16)
    return high, (x - high.astype(f32)).astype(bf16)


def one(a, b, dims):
    return lax.dot_general(a, b, dims, preferred_element_type=f32)


def dot(a, b, dims=NN):
    ah, al = a if isinstance(a, tuple) else split(a)
    bh, bl = b if isinstance(b, tuple) else split(b)
    total = one(ah, bh, dims)
    if bl is not None:
        total = total + one(ah, bl, dims)
    if al is not None:
        total = total + one(al, bh, dims)
    return total


def grid_iota(n):
    return (
        lax.broadcasted_iota(jnp.int32, (n, n), 0),
        lax.broadcasted_iota(jnp.int32, (n, n), 1),
    )


def inverse(lower, row, col):
    n = lower.shape[0]
    diff = row ^ col
    total = jnp.where(row == col, 1.0, jnp.where(diff == 1, -lower, 0.0))
    size = 2
    while size < n:
        part = jnp.where((diff >= size) & (diff < 2 * size), lower, 0.0)
        pieces = split(total)
        total = total - dot(pieces, dot(part, pieces))
        size *= 2
    return total


def merge_pair(first, second):
    d1, o1, a1 = first
    d2, o2, a2 = second
    s2 = split(d2)
    s1 = split(d1)
    return (
        d1 + d2 - dot(s1, s2),
        o1 + o2 - dot(o1, s2),
        a1 + a2 - dot(a2, s1, NT),
    )


def local_kernel(merge, core_ref, x_ref, wq_ref, wk_ref, wv_ref, wb_ref, bb_ref, do_ref, *refs):
    if merge:
        prior_ref, saved_ref, gates_ref, maps_ref, send_ref = refs
    else:
        saved_ref, gates_ref, maps_ref = refs
    core = core_ref[0]
    x = x_ref[...]
    q2 = one(x, wq_ref[...], NN)
    k2 = one(x, wk_ref[...], NN)
    v2 = one(x, wv_ref[...], NN)
    z = one(x, wb_ref[...], NN) + bb_ref[...]
    row, col = grid_iota(ROWS)
    lane = lax.broadcasted_iota(jnp.int32, (ROWS, WIDTH), 1)
    for head in range(2):
        cut = slice(head * WIDTH, (head + 1) * WIDTH)
        q, k, v = q2[:, cut], k2[:, cut], v2[:, cut]
        d_out = (do_ref[:, cut], None)
        rq = lax.rsqrt(jnp.sum(q * q, 1, keepdims=True) + EPSILON)
        rk = lax.rsqrt(jnp.sum(k * k, 1, keepdims=True) + EPSILON)
        qn = q * rq
        kn = k * rk
        logit = jnp.sum(jnp.where(lane == 2 * core + head, z, 0.0), 1, keepdims=True)
        beta = 2.0 * jax.nn.sigmoid(logit)
        ks = split(kn)
        gram = jnp.where(row > col, dot(ks, ks, NT), 0.0)
        scores = split(jnp.where(row >= col, dot(qn, ks, NT), 0.0))
        solve = split(inverse(beta * gram, row, col))
        wu = dot(solve, jnp.concatenate([beta * kn, beta * v], 1))
        wus = split(wu)
        gwu = dot(gram, wus)
        ke = kn - gwu[:, :WIDTH]
        ve = v - gwu[:, WIDTH:]
        pulled = dot(scores, d_out, TN)
        back = dot(solve, jnp.concatenate([kn, pulled], 1), TN)
        do_map = dot(wus, ks, TN)
        ws = (wus[0][:, :WIDTH], wus[1][:, :WIDTH])
        adjoint = dot(d_out, qn - dot(scores, ws), TN)
        saved_ref[head, 0] = qn
        saved_ref[head, 1] = kn
        saved_ref[head, 2] = ke
        saved_ref[head, 3] = ve
        saved_ref[head, 4] = back[:, :WIDTH]
        saved_ref[head, 5] = back[:, WIDTH:]
        gates_ref[head] = jnp.where(lane == 0, beta, jnp.where(lane == 1, rq, rk))
        maps_ref[head, 0] = do_map[:WIDTH]
        maps_ref[head, 1] = do_map[WIDTH:]
        maps_ref[head, 2] = adjoint
    if merge:
        early = core == 0
        for head in range(2):
            mine = [prior_ref[head, i] for i in range(3)]
            theirs = [maps_ref[head, i] for i in range(3)]
            first = [jnp.where(early, a, b) for a, b in zip(mine, theirs)]
            second = [jnp.where(early, b, a) for a, b in zip(mine, theirs)]
            step, offset, adjoint = merge_pair(first, second)
            for part in range(8):
                slot = head * 8 + part
                strip = slice(part * STRIP, (part + 1) * STRIP)
                send_ref[slot, :WIDTH] = step.astype(STATE)
                send_ref[slot, WIDTH : WIDTH + STRIP] = offset[strip].astype(STATE)
                send_ref[slot, WIDTH + STRIP :] = adjoint[strip].astype(STATE)


def local_pass(merge, core, x, wq, wk, wv, wb, bb, d_out, prior=None):
    whole = lambda shape: pl.BlockSpec(shape, lambda i, c: (0,) * len(shape))
    half = pl.BlockSpec((wq.shape[0], PAIR), lambda i, c: (0, c[0]))
    shapes = [
        jax.ShapeDtypeStruct((2, 6, ROWS, WIDTH), f32),
        jax.ShapeDtypeStruct((2, ROWS, WIDTH), f32),
        jax.ShapeDtypeStruct((2, 3, WIDTH, WIDTH), f32),
    ]
    args = [x, wq, wk, wv, wb, bb, d_out]
    specs = [whole(x.shape), half, half, half, whole(wb.shape), whole(bb.shape), whole(d_out.shape)]
    if merge:
        args.append(prior)
        specs.append(whole(prior.shape))
        shapes.append(jax.ShapeDtypeStruct((CHIPS, WIDTH + 2 * STRIP, WIDTH), STATE))
    return pl.pallas_call(
        functools.partial(local_kernel, merge),
        grid_spec=pltpu.PrefetchScalarGridSpec(
            num_scalar_prefetch=1,
            grid=(1,),
            in_specs=specs,
            out_specs=[whole(s.shape) for s in shapes],
        ),
        out_shape=shapes,
        compiler_params=pltpu.CompilerParams(vmem_limit_bytes=VMEM),
        cost_estimate=pl.CostEstimate(
            flops=8 * 10**9, bytes_accessed=6 * 10**6, transcendentals=0
        ),
        name="local_merge" if merge else "local",
    )(core, *args)


def scan_kernel(maps_ref, out_ref):
    state = jnp.zeros((STRIP, WIDTH), f32)
    adjoint = jnp.zeros((STRIP, WIDTH), f32)
    for i in range(CHIPS):
        j = CHIPS - 1 - i
        out_ref[i, :STRIP] = state.astype(STATE)
        out_ref[j, STRIP:] = adjoint.astype(STATE)
        if i < CHIPS - 1:
            offset = maps_ref[i, WIDTH : WIDTH + STRIP].astype(f32)
            own = maps_ref[j, WIDTH + STRIP :].astype(f32)
            state = state + offset - dot(state, maps_ref[i, :WIDTH].astype(f32))
            adjoint = adjoint + own - dot(adjoint, maps_ref[j, :WIDTH].astype(f32), NT)


def back_kernel(core_ref, own_ref, ogate_ref, omap_ref, odo_ref, sib_ref, sgate_ref, smap_ref,
                sdo_ref, scan_ref, grads_ref, dz_ref, share_ref):
    core = core_ref[0]
    early = core == 0
    row, col = grid_iota(ROWS)
    lane = lax.broadcasted_iota(jnp.int32, (ROWS, WIDTH), 1)
    units = ((own_ref, ogate_ref, odo_ref), (sib_ref, sgate_ref, sdo_ref))
    tails = [jnp.zeros((ROWS, WIDTH), f32) for _ in range(2)]
    shares = [jnp.zeros((ROWS, WIDTH), f32) for _ in range(2)]
    for head in range(2):
        block = scan_ref[head * 8 : (head + 1) * 8].astype(f32)
        start = block[:, :STRIP].reshape(WIDTH, WIDTH)
        later = block[:, STRIP:].reshape(WIDTH, WIDTH)
        mine = [omap_ref[head, i] for i in range(3)]
        theirs = [smap_ref[head, i] for i in range(3)]
        d1, o1 = (jnp.where(early, mine[i], theirs[i]) for i in (0, 1))
        d2, a2 = (jnp.where(early, theirs[i], mine[i]) for i in (0, 2))
        middle = start + o1 - dot(start, d1)
        inner = later + a2 - dot(later, d2, NT)
        states = (jnp.where(early, start, middle), jnp.where(early, middle, start))
        duals = (jnp.where(early, inner, later), jnp.where(early, later, inner))
        for unit in range(2):
            saved_ref, gate_ref, do_ref = units[unit]
            cut = slice(head * WIDTH, (head + 1) * WIDTH)
            d_out = do_ref[:, cut]
            qn, kn = saved_ref[head, 0], saved_ref[head, 1]
            gates = gate_ref[head]
            beta, rq, rk = gates[:, 0:1], gates[:, 1:2], gates[:, 2:3]
            state, dual = split(states[unit]), split(duals[unit])
            error = saved_ref[head, 3] - dot(saved_ref[head, 2], state, NT)
            update = split(beta * error)
            y = saved_ref[head, 5] + dot(saved_ref[head, 4], dual, NT)
            dv = beta * y
            dvs = split(dv)
            ks, qs = split(kn), split(qn)
            dm = split(jnp.where(row >= col, dot((d_out, None), update, NT), 0.0))
            dn = split(jnp.where(row > col, dot(dvs, update, NT), 0.0))
            dqn = dot((d_out, None), state) + dot(dm, ks)
            dkn = (
                dot(dm, qs, TN)
                + dot(update, dual)
                - dot(dn, ks)
                - dot(dn, ks, TN)
                - dot(dvs, state)
            )
            dq = rq * (dqn - qn * jnp.sum(qn * dqn, 1, keepdims=True))
            dk = rk * (dkn - kn * jnp.sum(kn * dkn, 1, keepdims=True))
            dz = jnp.sum(y * error, 1, keepdims=True) * beta * (1.0 - 0.5 * beta)
            for place, grad in enumerate((dq, dk, dv)):
                base = place * PAIR + head * WIDTH
                grads_ref[unit, :, base : base + WIDTH] = grad.astype(bf16)
            tails[unit] = tails[unit] + jnp.where((lane < 8) & (lane % 2 == head), dz, 0.0)
            shares[unit] = shares[unit] + jnp.where(lane == 2 * core + head, dz, 0.0)
    for unit in range(2):
        grads_ref[unit, :, 3 * PAIR :] = jnp.where(lane < 4, tails[unit], 0.0).astype(bf16)
        dz_ref[unit] = tails[unit]
        share_ref[unit] = shares[unit].astype(bf16)


def weights_kernel(own_ref, sib_ref, grads_ref, dz_ref, out_ref):
    total = one(own_ref[...], grads_ref[0], TN) + one(sib_ref[...], grads_ref[1], TN)
    tail = total[:, 3 * PAIR :]
    lane = lax.broadcasted_iota(jnp.int32, tail.shape, 1)
    sums = jnp.sum(dz_ref[0], 0, keepdims=True) + jnp.sum(dz_ref[1], 0, keepdims=True)
    tail = jnp.where(lane < 4, tail, sums)
    high = tail.astype(bf16).astype(f32)
    tail = jnp.where(lane % 4 < 2, high, tail - high)
    chips = out_ref.shape[0]
    rows = out_ref.shape[1]
    for chip in range(chips):
        cut = slice(chip * rows, (chip + 1) * rows)
        out_ref[chip, :, : 3 * PAIR] = total[cut, : 3 * PAIR].astype(bf16)
        out_ref[chip, :, 3 * PAIR :] = tail[cut].astype(bf16)


def input_kernel(place_ref, mine_ref, other_ref, share_ref, oshare_ref, wq_ref, wk_ref, wv_ref,
                 wb_ref, out_ref):
    core = place_ref[0]
    near = pl.ds(pl.multiple_of(core * PAIR, PAIR), PAIR)
    far = pl.ds(pl.multiple_of((1 - core) * PAIR, PAIR), PAIR)
    total = one(share_ref[...] + oshare_ref[...], wb_ref[...], NT)
    for place, w_ref in enumerate((wq_ref, wk_ref, wv_ref)):
        cut = slice(place * PAIR, (place + 1) * PAIR)
        total = total + one(mine_ref[:, cut], w_ref[:, near], NT)
        total = total + one(other_ref[:, cut], w_ref[:, far], NT)
    out_ref[0] = total.astype(bf16)


def per_device(tokens, w_query, w_key, w_value, w_beta, b_beta, d_out):
    depth = tokens.shape[1]
    index = lax.axis_index("seq")
    group = lax.axis_index("head")
    core = index % 2
    core_arr = core.reshape(1)
    seq = lax.axis_size("seq")
    ring = lax.axis_size("head")
    sibling = [(i, i ^ 1) for i in range(seq)]
    chips = [list(range(c, seq, 2)) for c in range(2)]

    def swap(x):
        return lax.ppermute(x, "seq", sibling)

    other_tokens = swap(tokens)
    do_mine = lax.dynamic_slice_in_dim(d_out, core * PAIR, PAIR, 1)
    do_other = swap(lax.dynamic_slice_in_dim(d_out, (1 - core) * PAIR, PAIR, 1))
    wb = jnp.pad(w_beta, ((0, 0), (0, WIDTH - w_beta.shape[1])))
    bb = jnp.pad(b_beta, (0, WIDTH - b_beta.shape[0])).reshape(1, WIDTH)

    own, own_gates, own_maps = local_pass(
        False, core_arr, tokens, w_query, w_key, w_value, wb, bb, do_mine
    )
    sib, sib_gates, sib_maps, send = local_pass(
        True, core_arr, other_tokens, w_query, w_key, w_value, wb, bb, do_other, own_maps
    )
    maps = lax.all_to_all(send, "seq", 0, 0, axis_index_groups=chips, tiled=True)
    scanned = pl.pallas_call(
        scan_kernel,
        out_shape=jax.ShapeDtypeStruct((CHIPS, 2 * STRIP, WIDTH), STATE),
        compiler_params=pltpu.CompilerParams(vmem_limit_bytes=VMEM),
        name="scan",
    )(maps)
    states = lax.all_to_all(scanned, "seq", 0, 0, axis_index_groups=chips, tiled=True)

    vmem = pl.BlockSpec(memory_space=pltpu.VMEM)
    grads, dz, share = pl.pallas_call(
        back_kernel,
        in_specs=[pl.BlockSpec(memory_space=pltpu.SMEM)] + [vmem] * 9,
        out_specs=[vmem] * 3,
        out_shape=[
            jax.ShapeDtypeStruct((2, ROWS, PACK), bf16),
            jax.ShapeDtypeStruct((2, ROWS, WIDTH), f32),
            jax.ShapeDtypeStruct((2, ROWS, WIDTH), bf16),
        ],
        compiler_params=pltpu.CompilerParams(vmem_limit_bytes=VMEM),
        name="back",
    )(core_arr, own, own_gates, own_maps, do_mine, sib, sib_gates, sib_maps, do_other, states)

    rows = depth // CHIPS
    tile = 2
    partial = pl.pallas_call(
        weights_kernel,
        grid=(CHIPS // tile,),
        in_specs=[
            pl.BlockSpec((ROWS, rows * tile), lambda i: (0, i)),
            pl.BlockSpec((ROWS, rows * tile), lambda i: (0, i)),
            pl.BlockSpec((2, ROWS, PACK), lambda i: (0, 0, 0)),
            pl.BlockSpec((2, ROWS, WIDTH), lambda i: (0, 0, 0)),
        ],
        out_specs=pl.BlockSpec((tile, rows, PACK), lambda i: (i, 0, 0)),
        out_shape=jax.ShapeDtypeStruct((CHIPS, rows, PACK), bf16),
        compiler_params=pltpu.CompilerParams(vmem_limit_bytes=VMEM),
        cost_estimate=pl.CostEstimate(
            flops=2 * 10**9, bytes_accessed=6 * 10**6, transcendentals=0
        ),
        name="weights",
    )(tokens, other_tokens, grads, dz)

    other_grads = swap(grads[1])
    other_share = swap(share[1])
    place = jnp.stack([core, group])
    width = depth // ring
    w_spec = pl.BlockSpec((width, w_query.shape[1]), lambda i, p: (i, 0))
    full = lambda shape: pl.BlockSpec(shape, lambda i, p: (0,) * len(shape))
    shifted = pl.pallas_call(
        input_kernel,
        grid_spec=pltpu.PrefetchScalarGridSpec(
            num_scalar_prefetch=1,
            grid=(ring,),
            in_specs=[
                full((ROWS, PACK)),
                full((ROWS, PACK)),
                full((ROWS, WIDTH)),
                full((ROWS, WIDTH)),
                w_spec,
                w_spec,
                w_spec,
                pl.BlockSpec((width, WIDTH), lambda i, p: (i, 0)),
            ],
            out_specs=pl.BlockSpec(
                (1, ROWS, width), lambda i, p: (lax.rem(i - p[1] + ring, ring), 0, 0)
            ),
        ),
        out_shape=jax.ShapeDtypeStruct((ring, ROWS, width), bf16),
        compiler_params=pltpu.CompilerParams(vmem_limit_bytes=VMEM),
        cost_estimate=pl.CostEstimate(
            flops=2 * 10**9, bytes_accessed=8 * 10**6, transcendentals=0
        ),
        name="inputs",
    )(place, grads[0], other_grads, share[0], other_share, w_query, w_key, w_value, wb)

    blocks = lax.all_to_all(partial, "seq", 0, 0, axis_index_groups=chips, tiled=True)
    arrived = [
        lax.ppermute(shifted[k], "head", [(i, (i + k) % ring) for i in range(ring)])
        for k in range(1, ring)
    ]
    d_x = shifted[0].astype(f32)
    for piece in arrived:
        d_x = d_x + piece.astype(f32)
    d_x = d_x.astype(bf16)

    summed = jnp.sum(blocks.astype(f32), 0)
    half = rows // 2
    keep = lax.dynamic_slice_in_dim(summed, core * half, half, 0)
    give = lax.dynamic_slice_in_dim(summed, (1 - core) * half, half, 0)
    got = swap(give)
    low = jnp.where(core == 0, keep, got)
    high = jnp.where(core == 0, got, keep)

    def joined(place):
        cut = slice(place * PAIR, (place + 1) * PAIR)
        return jnp.concatenate([low[:, cut], high[:, cut]], 1)

    def tail(base):
        def pick(side):
            part = side[:, 3 * PAIR + base : 3 * PAIR + base + 4]
            return part[:, :2] + part[:, 2:]

        return jnp.concatenate([pick(low), pick(high)], 1)

    return (d_x, joined(0), joined(1), joined(2), tail(0), tail(4)[0])


def solution(mesh):
    columns = P(None, "head")
    both = P("seq", "head")
    return jax.shard_map(
        per_device,
        mesh=mesh,
        in_specs=(P("seq", None), columns, columns, columns, columns, P("head"), both),
        out_specs=(both, both, both, both, both, P("head")),
        check_vma=False,
    )
```

```python
import functools

import jax
import jax.numpy as jnp
from jax import lax
from jax.experimental import pallas as pl
from jax.experimental.pallas import tpu as pltpu
from jax.sharding import PartitionSpec as P

EPSILON = 1e-06
WIDTH = 128
ROWS = 256
PAIR = 2 * WIDTH
SIDE = 4
PACK = 3 * PAIR
FULL = PACK + WIDTH
VMEM = 24 * 2**20
BIG = 50 * 2**20
SLAB = 16
f32 = jnp.float32
bf16 = jnp.bfloat16
STATE = jnp.bfloat16
BASE = 8

NN = (((1,), (0,)), ((), ()))
NT = (((1,), (1,)), ((), ()))
TN = (((0,), (0,)), ((), ()))


def split(x):
    high = x.astype(bf16)
    return high, (x - high.astype(f32)).astype(bf16)


def one(a, b, dims):
    return lax.dot_general(a, b, dims, preferred_element_type=f32)


def dot(a, b, dims=NN):
    ah, al = a if isinstance(a, tuple) else split(a)
    bh, bl = b if isinstance(b, tuple) else split(b)
    total = one(ah, bh, dims)
    if bl is not None:
        total = total + one(ah, bl, dims)
    if al is not None:
        total = total + one(al, bh, dims)
    return total


def grid_iota(n):
    return (
        lax.broadcasted_iota(jnp.int32, (n, n), 0),
        lax.broadcasted_iota(jnp.int32, (n, n), 1),
    )


def inverses(lowers, row, col):
    n = lowers[0].shape[0]
    diff = row ^ col
    near = diff < BASE
    lane = lax.broadcasted_iota(jnp.int32, (BASE, n), 1) % BASE
    rank = lax.broadcasted_iota(jnp.int32, (BASE, n), 0)
    totals = []
    for lower in lowers:
        packed = jnp.where(near, lower, 0.0).reshape(n // BASE, BASE, n).sum(0)
        solved = jnp.where(lane == rank, 1.0, 0.0)
        for j in range(BASE - 1):
            factor = jnp.where(lane == j, packed, 0.0)
            if j:
                factor = pltpu.roll(factor, n - j, 1)
            step = 1
            while step < BASE:
                factor = factor + pltpu.roll(factor, step, 1)
                step *= 2
            solved = solved - factor * solved[j : j + 1, :]
        wide = jnp.broadcast_to(solved[None], (n // BASE, BASE, n)).reshape(n, n)
        totals.append(jnp.where(near, wide, 0.0))
    size = BASE
    while size < n // 2:
        mask = (diff >= size) & (diff < 2 * size)
        pieces = [split(t) for t in totals]
        inner = [dot(jnp.where(mask, w, 0.0), p) for w, p in zip(lowers, pieces)]
        totals = [t - dot(p, i) for t, p, i in zip(totals, pieces, inner)]
        size *= 2
    h = n // 2
    firsts = [split(t[:h, :h]) for t in totals]
    lasts = [split(t[h:, h:]) for t in totals]
    inner = [dot(w[h:, :h], p) for w, p in zip(lowers, firsts)]
    corners = [-dot(p, i) for p, i in zip(lasts, inner)]
    return [
        jnp.concatenate([t[:h], jnp.concatenate([c, t[h:, h:]], 1)], 0)
        for t, c in zip(totals, corners)
    ]


def merge_pair(first, second):
    d1, o1, a1 = first
    d2, o2, a2 = second
    s2 = split(d2)
    s1 = split(d1)
    return (
        d1 + d2 - dot(s1, s2),
        o1 + o2 - dot(o1, s2),
        a1 + a2 - dot(a2, s1, NT),
    )


def project(x, wq_ref, wk_ref, wv_ref, wb_ref):
    return [
        one(x, wq_ref[...], NN),
        one(x, wk_ref[...], NN),
        one(x, wv_ref[...], NN),
        one(x, wb_ref[...], NT),
    ]


def project_kernel(place_ref, x_ref, wq_ref, wk_ref, wv_ref, wb_ref, out_ref):
    parts = project(x_ref[...], wq_ref, wk_ref, wv_ref, wb_ref)
    for place, part in enumerate(parts):
        out_ref[:, place * PAIR : place * PAIR + part.shape[1]] = part


def local_kernel(core_ref, own_ref, x_ref, wq_ref, wk_ref, wv_ref, wb_ref, do_ref, sdo_ref, bb_ref,
                 saved_ref, solve_ref, gates_ref, maps_ref, send_ref):
    core = core_ref[0]
    row, col = grid_iota(ROWS)
    lane = lax.broadcasted_iota(jnp.int32, (ROWS, WIDTH), 1)
    own = [own_ref[:, i * PAIR : (i + 1) * PAIR] for i in range(3)]
    heads = wb_ref.shape[0]
    own.append(own_ref[:, 3 * PAIR : 3 * PAIR + heads])
    sib = project(x_ref[...], wq_ref, wk_ref, wv_ref, wb_ref)
    narrow = lax.broadcasted_iota(jnp.int32, (ROWS, heads), 1)
    cuts = (slice(0, WIDTH), slice(WIDTH, PAIR))
    cases = [(unit, head) for unit in range(2) for head in range(2)]
    every = range(4)
    parts = (own, sib)
    d_outs = [((do_ref, sdo_ref)[u][:, cuts[h]], None) for u, h in cases]
    vs = [parts[u][2][:, cuts[h]] for u, h in cases]
    qns, kns, betas = [], [], []
    for unit, head in cases:
        q, k = (parts[unit][i][:, cuts[head]] for i in (0, 1))
        rq = lax.rsqrt(jnp.sum(q * q, 1, keepdims=True) + EPSILON)
        rk = lax.rsqrt(jnp.sum(k * k, 1, keepdims=True) + EPSILON)
        z = parts[unit][3]
        logit = jnp.sum(jnp.where(narrow == 2 * core + head, z, 0.0), 1, keepdims=True)
        beta = 2.0 * jax.nn.sigmoid(logit + bb_ref[2 * core + head])
        case = unit * 2 + head
        gates_ref[case] = jnp.where(lane == 0, beta, jnp.where(lane == 1, rq, rk))
        qns.append(q * rq)
        kns.append(k * rk)
        betas.append(beta)
    for i in every:
        saved_ref[i, 0] = qns[i]
        saved_ref[i, 1] = kns[i]
    ks = [split(kn) for kn in kns]
    grams = [jnp.where(row > col, dot(k, k, NT), 0.0) for k in ks]
    scores = [split(jnp.where(row >= col, dot(q, k, NT), 0.0)) for q, k in zip(qns, ks)]
    solves = inverses([beta * gram for beta, gram in zip(betas, grams)], row, col)
    solves = [split(x) for x in solves]
    wus = [
        split(dot(solves[i], jnp.concatenate([betas[i] * kns[i], betas[i] * vs[i]], 1)))
        for i in every
    ]
    pairs = [dot(wus[i], ks[i], TN) for i in every]
    reads = [
        qns[i] - dot(scores[i], (wus[i][0][:, :WIDTH], wus[i][1][:, :WIDTH])) for i in every
    ]
    adjoints = [dot(d_outs[i], reads[i], TN) for i in every]
    for i in every:
        maps_ref[i, 0] = pairs[i][:WIDTH]
        maps_ref[i, 1] = pairs[i][WIDTH:]
        maps_ref[i, 2] = adjoints[i]
        saved_ref[i, 2] = vs[i]
        for half in range(2):
            solve_ref[i, half] = solves[i][half]
            solve_ref[i, 2 + half] = wus[i][half]
    early = core == 0
    for head in range(2):
        mine = (pairs[head][:WIDTH], pairs[head][WIDTH:], adjoints[head])
        theirs = (pairs[2 + head][:WIDTH], pairs[2 + head][WIDTH:], adjoints[2 + head])
        first = [jnp.where(early, a, b) for a, b in zip(mine, theirs)]
        second = [jnp.where(early, b, a) for a, b in zip(mine, theirs)]
        step, offset, adjoint = merge_pair(first, second)
        send_ref[head, 0] = step.astype(STATE)
        send_ref[head, 1] = offset.astype(STATE)
        send_ref[head, 2] = adjoint.astype(STATE)


def by_core(kernel, name, core, args, halves, shapes, flops, nbytes, vmem):
    def whole(shape):
        return pl.BlockSpec(shape, lambda i, c: (0,) * len(shape))

    specs = [
        pl.BlockSpec((a.shape[0], PAIR), lambda i, c: (0, c[0]))
        if n in halves
        else (whole(a.shape) if a.ndim > 1 else pl.BlockSpec(memory_space=pltpu.SMEM))
        for n, a in enumerate(args)
    ]
    return pl.pallas_call(
        kernel,
        grid_spec=pltpu.PrefetchScalarGridSpec(
            num_scalar_prefetch=1,
            grid=(1,),
            in_specs=specs,
            out_specs=[whole(s.shape) for s in shapes],
        ),
        out_shape=shapes,
        compiler_params=pltpu.CompilerParams(vmem_limit_bytes=vmem),
        cost_estimate=pl.CostEstimate(flops=flops, bytes_accessed=nbytes, transcendentals=0),
        name=name,
    )(core, *args)


def extra_kernel(core_ref, saved_ref, solve_ref, do_ref, sdo_ref, out_ref):
    row, col = grid_iota(ROWS)
    every = range(4)
    d_outs = [((do_ref, sdo_ref)[i // 2][:, (i % 2) * WIDTH : (i % 2 + 1) * WIDTH], None) for i in every]
    kns = [saved_ref[i, 1] for i in every]
    ks = [split(kn) for kn in kns]
    grams = [jnp.where(row > col, dot(k, k, NT), 0.0) for k in ks]
    scores = [jnp.where(row >= col, dot(saved_ref[i, 0], ks[i], NT), 0.0) for i in every]
    gwus = [dot(grams[i], (solve_ref[i, 2], solve_ref[i, 3])) for i in every]
    pulled = [dot(scores[i], d_outs[i], TN) for i in every]
    backs = [
        dot((solve_ref[i, 0], solve_ref[i, 1]), jnp.concatenate([kns[i], pulled[i]], 1), TN)
        for i in every
    ]
    for i in every:
        out_ref[i, 0] = kns[i] - gwus[i][:, :WIDTH]
        out_ref[i, 1] = saved_ref[i, 2] - gwus[i][:, WIDTH:]
        out_ref[i, 2] = backs[i][:, :WIDTH]
        out_ref[i, 3] = backs[i][:, WIDTH:]


def flip_kernel(own_ref, sib_ref, after_ref, out_ref):
    step = pl.program_id(0)
    rows = out_ref.shape[3]
    for source, cut in ((own_ref, slice(0, ROWS)), (sib_ref, slice(ROWS, 2 * ROWS))):
        turned = source[...].T
        for j in range(SIDE):
            base = 2 * j * rows
            out_ref[0, j, step, :, cut] = turned[base : base + rows]
            out_ref[1, step, j, :, cut] = turned[base + rows : base + 2 * rows]


def compose_kernel(place_ref, own_ref, one_ref, two_ref, three_ref, after_ref, extra_ref, span_ref, *refs):
    sends, maps_ref = refs[:-1], refs[-1]
    y, x = place_ref[1], place_ref[2]
    for k, ref in enumerate((own_ref, one_ref, two_ref, three_ref)):
        maps_ref[lax.rem(y - k + SIDE, SIDE)] = ref[...]
    last = y == SIDE - 1
    for head in range(2):
        a, b, c, d = ([maps_ref[j, head, i].astype(f32) for i in range(3)] for j in range(SIDE))
        low = merge_pair(a, b)
        high = merge_pair(c, d)
        extra = merge_pair(
            [jnp.where(last, p, q) for p, q in zip(low, b)],
            [jnp.where(last, p, q) for p, q in zip(c, high)],
        )
        step, offset, adjoint = merge_pair(low, high)
        for i in (0, 1):
            before = jnp.where(y == 1, a[i], jnp.where(y == 2, low[i], extra[i]))
            span_ref[head, i] = jnp.where(y == 0, 0.0, before)
        for i, place in ((0, 2), (2, 3)):
            behind = jnp.where(y == 2, d[i], jnp.where(y == 1, high[i], extra[i]))
            span_ref[head, place] = jnp.where(last, 0.0, behind)
        for k, out in enumerate(sends, 1):
            out[head, 0] = step.astype(STATE)
            out[head, 1] = jnp.where(x + k < SIDE, offset, adjoint).astype(STATE)


def back_kernel(place_ref, saved_ref, extra_ref, gates_ref, maps_ref, do_ref, sdo_ref, span_ref, one_ref,
                two_ref, three_ref, grads_ref, sums_ref):
    core, x = place_ref[0], place_ref[2]
    rows_of = {1: one_ref, 2: two_ref, 3: three_ref}
    early = core == 0
    row, col = grid_iota(ROWS)
    lane = lax.broadcasted_iota(jnp.int32, (ROWS, WIDTH), 1)
    rank = lax.broadcasted_iota(jnp.int32, (SLAB, WIDTH), 0)
    shares = [jnp.zeros((ROWS, WIDTH), f32) for _ in range(2)]
    sums = jnp.zeros((SLAB, WIDTH), f32)
    for head in range(2):
        start = jnp.zeros((WIDTH, WIDTH), f32)
        later = jnp.zeros((WIDTH, WIDTH), f32)
        for k in (3, 2, 1):
            moved = start + rows_of[k][head, 1].astype(f32)
            if k < 3:
                moved = moved - dot(start, (rows_of[k][head, 0], None))
            start = jnp.where(x >= k, moved, start)
        for k in (1, 2, 3):
            moved = later + rows_of[k][head, 1].astype(f32)
            if k > 1:
                moved = moved - dot(later, (rows_of[k][head, 0], None), NT)
            later = jnp.where(x < k, moved, later)
        start = start + span_ref[head, 1] - dot(start, span_ref[head, 0])
        later = later + span_ref[head, 3] - dot(later, span_ref[head, 2], NT)
        mine = [maps_ref[head, i] for i in range(3)]
        theirs = [maps_ref[2 + head, i] for i in range(3)]
        d1, o1 = (jnp.where(early, mine[i], theirs[i]) for i in (0, 1))
        d2, a2 = (jnp.where(early, theirs[i], mine[i]) for i in (0, 2))
        middle = start + o1 - dot(start, d1)
        inner = later + a2 - dot(later, d2, NT)
        states = (jnp.where(early, start, middle), jnp.where(early, middle, start))
        duals = (jnp.where(early, inner, later), jnp.where(early, later, inner))
        for unit in range(2):
            case = 2 * unit + head
            d_out = (do_ref, sdo_ref)[unit][:, head * WIDTH : (head + 1) * WIDTH]
            qn, kn = saved_ref[case, 0], saved_ref[case, 1]
            gates = gates_ref[case]
            beta, rq, rk = gates[:, 0:1], gates[:, 1:2], gates[:, 2:3]
            state, dual = split(states[unit]), split(duals[unit])
            error = extra_ref[case, 1] - dot(extra_ref[case, 0], state, NT)
            y = extra_ref[case, 3] + dot(extra_ref[case, 2], dual, NT)
            update = split(beta * error)
            dv = beta * y
            dvb = dv.astype(bf16)
            ks, qs = split(kn), split(qn)
            pulls = jnp.concatenate([d_out, dvb], 0)
            products = dot((pulls, None), update, NT)
            dm = jnp.where(row >= col, products[:ROWS], 0.0).astype(bf16)
            dn = jnp.where(row > col, products[ROWS:], 0.0).astype(bf16)
            lefts = dot((jnp.concatenate([dm, dn], 0), None), ks)
            rights = dot((pulls, None), state)
            both = tuple(jnp.concatenate([a, b], 0) for a, b in zip(qs, ks))
            dqn = rights[:ROWS] + lefts[:ROWS]
            dkn = (
                dot((jnp.concatenate([dm, -dn], 0), None), both, TN)
                + dot((update[0], None), dual)
                - lefts[ROWS:]
                - rights[ROWS:]
            )
            dq = rq * (dqn - qn * jnp.sum(qn * dqn, 1, keepdims=True))
            dk = rk * (dkn - kn * jnp.sum(kn * dkn, 1, keepdims=True))
            dz = jnp.sum(y * error, 1, keepdims=True) * beta * (1.0 - 0.5 * beta)
            for place, grad in enumerate((dq, dk, dv)):
                base = place * PAIR + head * WIDTH
                grads_ref[unit, :, base : base + WIDTH] = grad.astype(bf16)
            shares[unit] = shares[unit] + jnp.where(lane == 2 * core + head, dz, 0.0)
            sums = sums + jnp.where(rank == 4 + 2 * core + head, jnp.sum(dz, 0, keepdims=True), 0.0)
    for unit in range(2):
        grads_ref[unit, :, PACK:] = shares[unit].astype(bf16)
    sums_ref[...] = sums


def weights_kernel(away, place_ref, flipped_ref, grads_ref, sums_ref, *outs):
    rows = flipped_ref.shape[3]
    span = SIDE * rows
    grads = grads_ref[:, :, :PACK].reshape(2 * ROWS, PACK)
    shares = grads_ref[:, :, PACK:].reshape(2 * ROWS, WIDTH).T[:SLAB]
    lefts = [
        flipped_ref[0, lax.rem(place_ref[4 + away] + k, SIDE)].reshape(span, 2 * ROWS)
        for k in range(SIDE)
    ]
    lefts = jnp.concatenate(lefts, 0)
    total = one(lefts, grads, NN).astype(bf16)
    high, low = split(one(shares, lefts, NT) + sums_ref[:, 0:1])
    for k in range(SIDE):
        cut = slice(k * span, (k + 1) * span)
        outs[k][:span] = total[cut]
        outs[k][span:, :span] = high[:, cut]
        outs[k][span:, span : 2 * span] = low[:, cut]
        outs[k][span:, 2 * span :] = jnp.zeros((SLAB, PACK - 2 * span), bf16)
    if away:
        outs[SIDE][...] = grads_ref[1]


def weights_pass(name, away, place, flipped, grads, sums):
    rows = flipped.shape[3]
    shapes = [jax.ShapeDtypeStruct((SIDE * rows + SLAB, PACK), bf16)] * SIDE
    if away:
        shapes.append(jax.ShapeDtypeStruct(grads.shape[1:], bf16))

    def whole(shape):
        return pl.BlockSpec(shape, lambda k, p: (0,) * len(shape))

    return pl.pallas_call(
        functools.partial(weights_kernel, away),
        grid_spec=pltpu.PrefetchScalarGridSpec(
            num_scalar_prefetch=1,
            grid=(1,),
            in_specs=[
                pl.BlockSpec(
                    (1,) + flipped.shape[1:],
                    lambda k, p: (1 - p[0] if away else p[0], 0, 0, 0, 0),
                ),
                whole(grads.shape),
                whole(sums.shape),
            ],
            out_specs=[whole(s.shape) for s in shapes],
        ),
        out_shape=shapes,
        compiler_params=pltpu.CompilerParams(vmem_limit_bytes=VMEM),
        cost_estimate=pl.CostEstimate(flops=10**9, bytes_accessed=4 * 10**6, transcendentals=0),
        name=name,
    )(place, flipped, grads, sums)


def fair_sum(terms):
    return (terms[0] + terms[3]) + (terms[1] + terms[2])


def middle_kernel(place_ref, *refs):
    inputs, outs = refs[: 2 * SIDE], refs[2 * SIDE + 1 :]
    base = place_ref[5]
    rows = outs[0].shape[1] - SLAB
    span = SIDE * rows
    for pair in range(2):
        group = inputs[pair * SIDE : (pair + 1) * SIDE]
        slab = fair_sum(
            [ref[span:, :span].astype(f32) + ref[span:, span : 2 * span].astype(f32) for ref in group]
        )
        for k in range(SIDE):
            slot = lax.rem(base + k, SIDE)
            place = pl.ds(pl.multiple_of(slot * rows, rows), rows)
            total = group[0][place, :].astype(f32)
            for ref in group[1:]:
                total = total + ref[place, :].astype(f32)
            kind = outs[k].dtype
            outs[k][pair, :rows] = total.astype(kind)
            turned = pltpu.roll(slab, lax.rem(span - slot * rows, span), 1)[:, :WIDTH]
            high = turned.astype(bf16).astype(f32)
            outs[k][pair, rows:, :WIDTH] = high.astype(kind)
            outs[k][pair, rows:, WIDTH : 2 * WIDTH] = (turned - high).astype(bf16).astype(kind)
            outs[k][pair, rows:, 2 * WIDTH :] = jnp.zeros((SLAB, PACK - 2 * WIDTH), kind)


def total_kernel(core_ref, own_ref, one_ref, two_ref, three_ref, *outs):
    early = core_ref[0] == 0
    rows = own_ref.shape[1] - SLAB
    sums = []
    tails = []
    refs = (own_ref, one_ref, two_ref, three_ref)
    for pair in range(2):
        total = own_ref[pair, :rows]
        for ref in refs[1:]:
            total = total + ref[pair, :rows].astype(f32)
        sums.append(total)
        slabs = [ref[pair, rows:, : 2 * WIDTH].astype(f32) for ref in refs]
        tails.append(fair_sum([t[:, :WIDTH] + t[:, WIDTH:] for t in slabs]))
    outs[3][...] = tails[0] + tails[1]
    low = jnp.where(early, sums[0], sums[1])
    high = jnp.where(early, sums[1], sums[0])
    for place, out in enumerate(outs[:3]):
        cut = slice(place * PAIR, (place + 1) * PAIR)
        out[:, :PAIR] = low[:, cut]
        out[:, PAIR:] = high[:, cut]


def call(name, kernel, scalars, args, shapes, scratch=(), idle=(), flops=0, nbytes=0):
    def whole(shape):
        return pl.BlockSpec(shape, lambda i, p: (0,) * len(shape))

    return pl.pallas_call(
        kernel,
        grid_spec=pltpu.PrefetchScalarGridSpec(
            num_scalar_prefetch=1,
            grid=(1,),
            in_specs=[whole(a.shape) for a in args]
            + [pl.BlockSpec(memory_space=pl.ANY)] * len(idle),
            out_specs=[whole(s.shape) for s in shapes],
            scratch_shapes=list(scratch),
        ),
        out_shape=shapes,
        compiler_params=pltpu.CompilerParams(vmem_limit_bytes=VMEM),
        cost_estimate=pl.CostEstimate(flops=flops, bytes_accessed=nbytes, transcendentals=0),
        name=name,
    )(scalars, *args, *idle)


def input_kernel(place_ref, mine_ref, other_ref, wq_ref, wk_ref, wv_ref, wb_ref, after_ref, *outs):
    core, step = place_ref[0], pl.program_id(0)
    near = pl.ds(pl.multiple_of(core * PAIR, PAIR), PAIR)
    far = pl.ds(pl.multiple_of((1 - core) * PAIR, PAIR), PAIR)
    shares = (mine_ref[0, :, PACK:] + other_ref[:, PACK:])[:, : wb_ref.shape[0]]
    total = one(shares, wb_ref[...], NN)
    for place, w_ref in enumerate((wq_ref, wk_ref, wv_ref)):
        cut = slice(place * PAIR, (place + 1) * PAIR)
        total = total + one(mine_ref[0, :, cut], w_ref[:, near], NT)
        total = total + one(other_ref[:, cut], w_ref[:, far], NT)
    total = total.astype(bf16)
    for k, out in enumerate(outs):

        @pl.when(step == k)
        def _():
            out[...] = total


def per_device(tokens, w_query, w_key, w_value, w_beta, b_beta, d_out):
    depth = tokens.shape[1]
    index = lax.axis_index("seq")
    group = lax.axis_index("head")
    core = index % 2
    chip = index // 2
    y, x = chip % SIDE, chip // SIDE
    first, second = jnp.where(core == 0, y, x), jnp.where(core == 0, x, y)
    place = jnp.stack([core, y, x, group, first, second])
    seq = lax.axis_size("seq")
    ring = lax.axis_size("head")
    sibling = [(i, i ^ 1) for i in range(seq)]

    def swap(x):
        return lax.ppermute(x, "seq", sibling)

    other_tokens = swap(tokens)
    do_other = swap(d_out)
    wb = w_beta.T

    (projected,) = by_core(
        project_kernel,
        "project",
        place,
        [tokens, w_query, w_key, w_value, wb],
        (1, 2, 3),
        [jax.ShapeDtypeStruct((ROWS, PACK + WIDTH), f32)],
        10**9,
        5 * 10**6,
        BIG,
    )
    saved, solved, gates, own_maps, send = by_core(
        local_kernel,
        "local",
        place,
        [projected, other_tokens, w_query, w_key, w_value, wb, d_out, do_other, b_beta],
        (2, 3, 4, 6, 7),
        [
            jax.ShapeDtypeStruct((4, 3, ROWS, WIDTH), f32),
            jax.ShapeDtypeStruct((4, 4, ROWS, ROWS), bf16),
            jax.ShapeDtypeStruct((4, ROWS, WIDTH), f32),
            jax.ShapeDtypeStruct((4, 3, WIDTH, WIDTH), f32),
            jax.ShapeDtypeStruct((2, 3, WIDTH, WIDTH), STATE),
        ],
        10**10,
        10**7,
        BIG,
    )
    (extra,) = by_core(
        extra_kernel,
        "extra",
        place,
        [saved, solved, d_out, do_other],
        (2, 3),
        [jax.ShapeDtypeStruct((4, 4, ROWS, WIDTH), f32)],
        10**10,
        5 * 10**6,
        VMEM,
    )
    idle = pl.BlockSpec(memory_space=pl.ANY)

    def along(k, axis):
        route = []
        for i in range(seq):
            x, y, c = i // (2 * SIDE), i // 2 % SIDE, i % 2
            if axis(c):
                x = (x + k) % SIDE
            else:
                y = (y + k) % SIDE
            route.append((i, (x * SIDE + y) * 2 + c))
        return route

    def shift(block, k, axis):
        return lax.ppermute(block, "seq", along(k, axis))

    rows = depth // seq
    block = depth // SIDE
    layout = (2, SIDE, SIDE, rows, 2 * ROWS)
    flipped = pl.pallas_call(
        flip_kernel,
        grid=(SIDE,),
        in_specs=[pl.BlockSpec((ROWS, block), lambda i: (0, i))] * 2 + [idle],
        out_specs=pl.BlockSpec(layout, lambda i: (0,) * 5),
        out_shape=jax.ShapeDtypeStruct(layout, bf16),
        compiler_params=pltpu.CompilerParams(vmem_limit_bytes=VMEM),
        cost_estimate=pl.CostEstimate(flops=0, bytes_accessed=8 * 10**6, transcendentals=0),
        name="flip",
    )(tokens, other_tokens, send)

    far = {k: shift(send, k, lambda c: False) for k in (1, 3, 2)}
    part = (2, 2, WIDTH, WIDTH)
    span, *sends = call(
        "compose",
        compose_kernel,
        place,
        [send, far[1], far[2], far[3]],
        [jax.ShapeDtypeStruct((2, 4, WIDTH, WIDTH), f32)]
        + [jax.ShapeDtypeStruct(part, STATE)] * (SIDE - 1),
        scratch=[pltpu.VMEM((SIDE, 2, 3, WIDTH, WIDTH), STATE)],
        idle=[flipped, extra],
        flops=10**9,
    )
    far = {k: shift(sends[k - 1], k, lambda c: True) for k in (1, 3, 2)}

    grads, sums = by_core(
        back_kernel,
        "back",
        place,
        [saved, extra, gates, own_maps, d_out, do_other, span, far[1], far[2], far[3]],
        (4, 5),
        [
            jax.ShapeDtypeStruct((2, ROWS, FULL), bf16),
            jax.ShapeDtypeStruct((SLAB, WIDTH), f32),
        ],
        4 * 10**9,
        8 * 10**6,
        VMEM,
    )

    def across(k):
        return [(i, j ^ 1) for i, j in along(k, lambda c: c == 0)]

    *give, relay = weights_pass("give", 1, place, flipped, grads, sums)
    given = [lax.ppermute(give[k], "seq", across(k)) for k in (0, 1, 3, 2)]
    other_grads = swap(relay)
    keep = weights_pass("keep", 0, place, flipped, grads, sums)
    kept = [keep[0]] + [shift(keep[k], k, lambda c: c == 1) for k in (1, 3, 2)]

    width = depth // ring

    def full(shape):
        return pl.BlockSpec(shape, lambda i, p: (0,) * len(shape))

    def rows_at(columns):
        return pl.BlockSpec((width, columns), lambda i, p: (lax.rem(i + p[3], ring), 0))

    shifted = pl.pallas_call(
        input_kernel,
        grid_spec=pltpu.PrefetchScalarGridSpec(
            num_scalar_prefetch=1,
            grid=(ring,),
            in_specs=[full((1, ROWS, FULL)), full((ROWS, FULL))]
            + [rows_at(w_query.shape[1])] * 3
            + [
                pl.BlockSpec((wb.shape[0], width), lambda i, p: (0, lax.rem(i + p[3], ring))),
                idle,
            ],
            out_specs=[full((ROWS, width))] * ring,
        ),
        out_shape=[jax.ShapeDtypeStruct((ROWS, width), bf16)] * ring,
        compiler_params=pltpu.CompilerParams(vmem_limit_bytes=VMEM),
        cost_estimate=pl.CostEstimate(
            flops=4 * 10**10, bytes_accessed=8 * 10**6, transcendentals=0
        ),
        name="inputs",
    )(place, grads, other_grads, w_query, w_key, w_value, wb, keep[1])

    arrived = [
        lax.ppermute(shifted[k], "head", [(i, (i + k) % ring) for i in range(ring)])
        for k in range(1, ring)
    ]
    d_x = shifted[0].astype(f32)
    for piece in arrived:
        d_x = d_x + piece.astype(f32)
    d_x = d_x.astype(bf16)

    message = (2, rows + SLAB, PACK)
    passed = call(
        "middle",
        middle_kernel,
        place,
        [*kept, *given],
        [jax.ShapeDtypeStruct(message, f32)]
        + [jax.ShapeDtypeStruct(message, bf16)] * (SIDE - 1),
        idle=[shifted[0]],
    )
    final = [shift(passed[k], k, lambda c: c == 0) for k in (1, 3, 2)]
    grad_query, grad_key, grad_value, tail = call(
        "total",
        total_kernel,
        place,
        [passed[0], *final],
        [jax.ShapeDtypeStruct((rows, 2 * PAIR), f32)] * 3
        + [jax.ShapeDtypeStruct((SLAB, WIDTH), f32)],
    )
    heads = w_beta.shape[1]
    grad_bbeta = jnp.where(core == 0, tail, swap(tail))[4 : 4 + heads, 0]
    return (d_x, grad_query, grad_key, grad_value, tail[:heads, :rows].T, grad_bbeta)


def solution(mesh):
    columns = P(None, "head")
    both = P("seq", "head")
    return jax.shard_map(
        per_device,
        mesh=mesh,
        in_specs=(P("seq", None), columns, columns, columns, columns, P("head"), both),
        out_specs=(both, both, both, both, both, P("head")),
        check_vma=False,
    )
```

```python
import functools

import jax
import jax.numpy as jnp
from jax import lax
from jax.experimental import pallas as pl
from jax.experimental.pallas import tpu as pltpu
from jax.sharding import PartitionSpec as P

EPSILON = 1e-06
WIDTH = 128
ROWS = 256
PAIR = 2 * WIDTH
SIDE = 4
PACK = 3 * PAIR
FULL = PACK + WIDTH
VMEM = 24 * 2**20
BIG = 50 * 2**20
CHUNK = 48
SLAB = 16
f32 = jnp.float32
bf16 = jnp.bfloat16
STATE = jnp.bfloat16
BASE = 8

NN = (((1,), (0,)), ((), ()))
NT = (((1,), (1,)), ((), ()))
TN = (((0,), (0,)), ((), ()))


def split(x):
    high = x.astype(bf16)
    return high, (x - high.astype(f32)).astype(bf16)


def one(a, b, dims):
    return lax.dot_general(a, b, dims, preferred_element_type=f32)


def dot(a, b, dims=NN):
    ah, al = a if isinstance(a, tuple) else split(a)
    bh, bl = b if isinstance(b, tuple) else split(b)
    total = one(ah, bh, dims)
    if bl is not None:
        total = total + one(ah, bl, dims)
    if al is not None:
        total = total + one(al, bh, dims)
    return total


def grid_iota(n):
    return (
        lax.broadcasted_iota(jnp.int32, (n, n), 0),
        lax.broadcasted_iota(jnp.int32, (n, n), 1),
    )


def inverses(lowers, row, col):
    n = lowers[0].shape[0]
    diff = row ^ col
    near = diff < BASE
    lane = lax.broadcasted_iota(jnp.int32, (BASE, n), 1) % BASE
    rank = lax.broadcasted_iota(jnp.int32, (BASE, n), 0)
    totals = []
    for lower in lowers:
        packed = jnp.where(near, lower, 0.0).reshape(n // BASE, BASE, n).sum(0)
        solved = jnp.where(lane == rank, 1.0, 0.0)
        for j in range(BASE - 1):
            factor = jnp.where(lane == j, packed, 0.0)
            if j:
                factor = pltpu.roll(factor, n - j, 1)
            step = 1
            while step < BASE:
                factor = factor + pltpu.roll(factor, step, 1)
                step *= 2
            solved = solved - factor * solved[j : j + 1, :]
        wide = jnp.broadcast_to(solved[None], (n // BASE, BASE, n)).reshape(n, n)
        totals.append(jnp.where(near, wide, 0.0))
    size = BASE
    while size < n // 2:
        mask = (diff >= size) & (diff < 2 * size)
        pieces = [split(t) for t in totals]
        inner = [dot(jnp.where(mask, w, 0.0), p) for w, p in zip(lowers, pieces)]
        totals = [t - dot(p, i) for t, p, i in zip(totals, pieces, inner)]
        size *= 2
    h = n // 2
    firsts = [split(t[:h, :h]) for t in totals]
    lasts = [split(t[h:, h:]) for t in totals]
    inner = [dot(w[h:, :h], p) for w, p in zip(lowers, firsts)]
    corners = [-dot(p, i) for p, i in zip(lasts, inner)]
    return [
        jnp.concatenate([t[:h], jnp.concatenate([c, t[h:, h:]], 1)], 0)
        for t, c in zip(totals, corners)
    ]


def merge_pair(first, second):
    d1, o1, a1 = first
    d2, o2, a2 = second
    s2 = split(d2)
    s1 = split(d1)
    return (
        d1 + d2 - dot(s1, s2),
        o1 + o2 - dot(o1, s2),
        a1 + a2 - dot(a2, s1, NT),
    )


def project(x, wq_ref, wk_ref, wv_ref, wb_ref):
    return [
        one(x, wq_ref[...], NN),
        one(x, wk_ref[...], NN),
        one(x, wv_ref[...], NN),
        one(x, wb_ref[...], NT),
    ]


def project_kernel(place_ref, x_ref, wq_ref, wk_ref, wv_ref, wb_ref, out_ref):
    parts = project(x_ref[...], wq_ref, wk_ref, wv_ref, wb_ref)
    for place, part in enumerate(parts):
        out_ref[:, place * PAIR : place * PAIR + part.shape[1]] = part


def local_kernel(core_ref, own_ref, x_ref, wq_ref, wk_ref, wv_ref, wb_ref, do_ref, sdo_ref, bb_ref,
                 saved_ref, solve_ref, gates_ref, maps_ref, send_ref):
    core = core_ref[0]
    row, col = grid_iota(ROWS)
    lane = lax.broadcasted_iota(jnp.int32, (ROWS, WIDTH), 1)
    own = [own_ref[:, i * PAIR : (i + 1) * PAIR] for i in range(3)]
    heads = wb_ref.shape[0]
    own.append(own_ref[:, 3 * PAIR : 3 * PAIR + heads])
    sib = project(x_ref[...], wq_ref, wk_ref, wv_ref, wb_ref)
    narrow = lax.broadcasted_iota(jnp.int32, (ROWS, heads), 1)
    cuts = (slice(0, WIDTH), slice(WIDTH, PAIR))
    cases = [(unit, head) for unit in range(2) for head in range(2)]
    every = range(4)
    parts = (own, sib)
    d_outs = [((do_ref, sdo_ref)[u][:, cuts[h]], None) for u, h in cases]
    vs = [parts[u][2][:, cuts[h]] for u, h in cases]
    qns, kns, betas = [], [], []
    for unit, head in cases:
        q, k = (parts[unit][i][:, cuts[head]] for i in (0, 1))
        rq = lax.rsqrt(jnp.sum(q * q, 1, keepdims=True) + EPSILON)
        rk = lax.rsqrt(jnp.sum(k * k, 1, keepdims=True) + EPSILON)
        z = parts[unit][3]
        logit = jnp.sum(jnp.where(narrow == 2 * core + head, z, 0.0), 1, keepdims=True)
        beta = 2.0 * jax.nn.sigmoid(logit + bb_ref[2 * core + head])
        case = unit * 2 + head
        gates_ref[case] = jnp.where(lane == 0, beta, jnp.where(lane == 1, rq, rk))
        qns.append(q * rq)
        kns.append(k * rk)
        betas.append(beta)
    for i in every:
        saved_ref[i, 0] = qns[i]
        saved_ref[i, 1] = kns[i]
    ks = [split(kn) for kn in kns]
    grams = [jnp.where(row > col, dot(k, k, NT), 0.0) for k in ks]
    scores = [split(jnp.where(row >= col, dot(q, k, NT), 0.0)) for q, k in zip(qns, ks)]
    solves = inverses([beta * gram for beta, gram in zip(betas, grams)], row, col)
    solves = [split(x) for x in solves]
    wus = [
        split(dot(solves[i], jnp.concatenate([betas[i] * kns[i], betas[i] * vs[i]], 1)))
        for i in every
    ]
    pairs = [dot(wus[i], ks[i], TN) for i in every]
    reads = [
        qns[i] - dot(scores[i], (wus[i][0][:, :WIDTH], wus[i][1][:, :WIDTH])) for i in every
    ]
    adjoints = [dot(d_outs[i], reads[i], TN) for i in every]
    for i in every:
        maps_ref[i, 0] = pairs[i][:WIDTH]
        maps_ref[i, 1] = pairs[i][WIDTH:]
        maps_ref[i, 2] = adjoints[i]
        saved_ref[i, 2] = vs[i]
        for half in range(2):
            solve_ref[i, half] = solves[i][half]
            solve_ref[i, 2 + half] = wus[i][half]
    early = core == 0
    for head in range(2):
        mine = (pairs[head][:WIDTH], pairs[head][WIDTH:], adjoints[head])
        theirs = (pairs[2 + head][:WIDTH], pairs[2 + head][WIDTH:], adjoints[2 + head])
        first = [jnp.where(early, a, b) for a, b in zip(mine, theirs)]
        second = [jnp.where(early, b, a) for a, b in zip(mine, theirs)]
        step, offset, adjoint = merge_pair(first, second)
        send_ref[head, 0] = step.astype(STATE)
        send_ref[head, 1] = offset.astype(STATE)
        send_ref[head, 2] = adjoint.astype(STATE)


def by_core(kernel, name, core, args, halves, shapes, flops, nbytes, vmem):
    def whole(shape):
        return pl.BlockSpec(shape, lambda i, c: (0,) * len(shape))

    specs = [
        pl.BlockSpec((a.shape[0], PAIR), lambda i, c: (0, c[0]))
        if n in halves
        else (whole(a.shape) if a.ndim > 1 else pl.BlockSpec(memory_space=pltpu.SMEM))
        for n, a in enumerate(args)
    ]
    return pl.pallas_call(
        kernel,
        grid_spec=pltpu.PrefetchScalarGridSpec(
            num_scalar_prefetch=1,
            grid=(1,),
            in_specs=specs,
            out_specs=[whole(s.shape) for s in shapes],
        ),
        out_shape=shapes,
        compiler_params=pltpu.CompilerParams(vmem_limit_bytes=vmem),
        cost_estimate=pl.CostEstimate(flops=flops, bytes_accessed=nbytes, transcendentals=0),
        name=name,
    )(core, *args)


def extra_kernel(core_ref, saved_ref, solve_ref, do_ref, sdo_ref, out_ref):
    row, col = grid_iota(ROWS)
    every = range(4)
    d_outs = [((do_ref, sdo_ref)[i // 2][:, (i % 2) * WIDTH : (i % 2 + 1) * WIDTH], None) for i in every]
    kns = [saved_ref[i, 1] for i in every]
    ks = [split(kn) for kn in kns]
    grams = [jnp.where(row > col, dot(k, k, NT), 0.0) for k in ks]
    scores = [jnp.where(row >= col, dot(saved_ref[i, 0], ks[i], NT), 0.0) for i in every]
    gwus = [dot(grams[i], (solve_ref[i, 2], solve_ref[i, 3])) for i in every]
    pulled = [dot(scores[i], d_outs[i], TN) for i in every]
    backs = [
        dot((solve_ref[i, 0], solve_ref[i, 1]), jnp.concatenate([kns[i], pulled[i]], 1), TN)
        for i in every
    ]
    for i in every:
        out_ref[i, 0] = kns[i] - gwus[i][:, :WIDTH]
        out_ref[i, 1] = saved_ref[i, 2] - gwus[i][:, WIDTH:]
        out_ref[i, 2] = backs[i][:, :WIDTH]
        out_ref[i, 3] = backs[i][:, WIDTH:]


def flip_kernel(own_ref, sib_ref, after_ref, out_ref):
    step = pl.program_id(0)
    rows = out_ref.shape[3]
    for source, cut in ((own_ref, slice(0, ROWS)), (sib_ref, slice(ROWS, 2 * ROWS))):
        turned = source[...].T
        for j in range(SIDE):
            base = 2 * j * rows
            out_ref[0, j, step, :, cut] = turned[base : base + rows]
            out_ref[1, step, j, :, cut] = turned[base + rows : base + 2 * rows]


def compose_kernel(place_ref, own_ref, one_ref, two_ref, three_ref, after_ref, extra_ref, span_ref, *refs):
    sends, maps_ref = refs[:-1], refs[-1]
    y, x = place_ref[1], place_ref[2]
    for k, ref in enumerate((own_ref, one_ref, two_ref, three_ref)):
        maps_ref[lax.rem(y - k + SIDE, SIDE)] = ref[...]
    last = y == SIDE - 1
    for head in range(2):
        a, b, c, d = ([maps_ref[j, head, i].astype(f32) for i in range(3)] for j in range(SIDE))
        low = merge_pair(a, b)
        high = merge_pair(c, d)
        extra = merge_pair(
            [jnp.where(last, p, q) for p, q in zip(low, b)],
            [jnp.where(last, p, q) for p, q in zip(c, high)],
        )
        step, offset, adjoint = merge_pair(low, high)
        for i in (0, 1):
            before = jnp.where(y == 1, a[i], jnp.where(y == 2, low[i], extra[i]))
            span_ref[head, i] = jnp.where(y == 0, 0.0, before)
        for i, place in ((0, 2), (2, 3)):
            behind = jnp.where(y == 2, d[i], jnp.where(y == 1, high[i], extra[i]))
            span_ref[head, place] = jnp.where(last, 0.0, behind)
        for k, out in enumerate(sends, 1):
            out[head, 0] = step.astype(STATE)
            out[head, 1] = jnp.where(x + k < SIDE, offset, adjoint).astype(STATE)


def back_kernel(place_ref, saved_ref, extra_ref, gates_ref, maps_ref, do_ref, sdo_ref, span_ref, one_ref,
                two_ref, three_ref, grads_ref, sums_ref):
    core, x = place_ref[0], place_ref[2]
    rows_of = {1: one_ref, 2: two_ref, 3: three_ref}
    early = core == 0
    row, col = grid_iota(ROWS)
    lane = lax.broadcasted_iota(jnp.int32, (ROWS, WIDTH), 1)
    rank = lax.broadcasted_iota(jnp.int32, (SLAB, WIDTH), 0)
    shares = [jnp.zeros((ROWS, WIDTH), f32) for _ in range(2)]
    sums = jnp.zeros((SLAB, WIDTH), f32)
    states, duals = [None] * 4, [None] * 4
    starts, laters = [], []
    for head in range(2):
        start = jnp.zeros((WIDTH, WIDTH), f32)
        later = jnp.zeros((WIDTH, WIDTH), f32)
        for k in (3, 2, 1):
            moved = start + rows_of[k][head, 1].astype(f32)
            if k < 3:
                moved = moved - dot(start, (rows_of[k][head, 0], None))
            start = jnp.where(x >= k, moved, start)
            m = SIDE - k
            moved = later + rows_of[m][head, 1].astype(f32)
            if m > 1:
                moved = moved - dot(later, (rows_of[m][head, 0], None), NT)
            later = jnp.where(x < m, moved, later)
        starts.append(start)
        laters.append(later)
    starts = [s + span_ref[h, 1] - dot(s, span_ref[h, 0]) for h, s in enumerate(starts)]
    laters = [s + span_ref[h, 3] - dot(s, span_ref[h, 2], NT) for h, s in enumerate(laters)]
    for head in range(2):
        mine = [maps_ref[head, i] for i in range(3)]
        theirs = [maps_ref[2 + head, i] for i in range(3)]
        d1, o1 = (jnp.where(early, mine[i], theirs[i]) for i in (0, 1))
        d2, a2 = (jnp.where(early, theirs[i], mine[i]) for i in (0, 2))
        start, later = starts[head], laters[head]
        middle = start + o1 - dot(start, d1)
        inner = later + a2 - dot(later, d2, NT)
        states[head] = split(jnp.where(early, start, middle))
        states[2 + head] = split(jnp.where(early, middle, start))
        duals[head] = split(jnp.where(early, inner, later))
        duals[2 + head] = split(jnp.where(early, later, inner))
    every = range(4)
    cuts = [slice((i % 2) * WIDTH, (i % 2 + 1) * WIDTH) for i in every]
    qns = [saved_ref[i, 0] for i in every]
    kns = [saved_ref[i, 1] for i in every]
    betas = [gates_ref[i, :, 0:1] for i in every]
    errors = [extra_ref[i, 1] - dot(extra_ref[i, 0], states[i], NT) for i in every]
    ys = [extra_ref[i, 3] + dot(extra_ref[i, 2], duals[i], NT) for i in every]
    updates = [split(b * e) for b, e in zip(betas, errors)]
    dvs = [(b * y).astype(bf16) for b, y in zip(betas, ys)]
    pulls = [
        (jnp.concatenate([(do_ref, sdo_ref)[i // 2][:, cuts[i]], dvs[i]], 0), None) for i in every
    ]
    products = [dot(p, u, NT) for p, u in zip(pulls, updates)]
    dms = [jnp.where(row >= col, p[:ROWS], 0.0).astype(bf16) for p in products]
    dns = [jnp.where(row > col, p[ROWS:], 0.0).astype(bf16) for p in products]
    qs, ks = [split(q) for q in qns], [split(k) for k in kns]
    lefts = [dot((jnp.concatenate([m, n], 0), None), k) for m, n, k in zip(dms, dns, ks)]
    rights = [dot(p, s) for p, s in zip(pulls, states)]
    both = [
        tuple(jnp.concatenate([a, b], 0) for a, b in zip(q, k)) for q, k in zip(qs, ks)
    ]
    turned = [
        dot((jnp.concatenate([m, -n], 0), None), t, TN) for m, n, t in zip(dms, dns, both)
    ]
    carried = [dot((u[0], None), d) for u, d in zip(updates, duals)]
    for i in every:
        unit, head = i // 2, i % 2
        dqn = rights[i][:ROWS] + lefts[i][:ROWS]
        dkn = turned[i] + carried[i] - lefts[i][ROWS:] - rights[i][ROWS:]
        qn, kn, beta = qns[i], kns[i], betas[i]
        dq = gates_ref[i, :, 1:2] * (dqn - qn * jnp.sum(qn * dqn, 1, keepdims=True))
        dk = gates_ref[i, :, 2:3] * (dkn - kn * jnp.sum(kn * dkn, 1, keepdims=True))
        dz = jnp.sum(ys[i] * errors[i], 1, keepdims=True) * beta * (1.0 - 0.5 * beta)
        for place, grad in enumerate((dq.astype(bf16), dk.astype(bf16), dvs[i])):
            base = place * PAIR + head * WIDTH
            grads_ref[unit, :, base : base + WIDTH] = grad
        shares[unit] = shares[unit] + jnp.where(lane == 2 * core + head, dz, 0.0)
        sums = sums + jnp.where(rank == 4 + 2 * core + head, jnp.sum(dz, 0, keepdims=True), 0.0)
    for unit in range(2):
        grads_ref[unit, :, PACK:] = shares[unit].astype(bf16)
    sums_ref[...] = sums


def weights_kernel(away, place_ref, flipped_ref, grads_ref, sums_ref, after_ref, *outs):
    rows = flipped_ref.shape[3]
    span = SIDE * rows
    grads = grads_ref[:, :, :PACK].reshape(2 * ROWS, PACK)
    shares = grads_ref[:, :, PACK:].reshape(2 * ROWS, WIDTH).T[:SLAB]
    lefts = [
        flipped_ref[0, lax.rem(place_ref[4 + away] + k, SIDE)].reshape(span, 2 * ROWS)
        for k in range(SIDE)
    ]
    lefts = jnp.concatenate(lefts, 0)
    total = one(lefts, grads, NN).astype(bf16)
    high, low = split(one(shares, lefts, NT) + sums_ref[:, 0:1])
    for k in range(SIDE):
        cut = slice(k * span, (k + 1) * span)
        outs[k][:span] = total[cut]
        last = span + SLAB
        outs[k][span:last, :span] = high[:, cut]
        outs[k][span:last, span : 2 * span] = low[:, cut]
        outs[k][span:last, 2 * span :] = jnp.zeros((SLAB, PACK - 2 * span), bf16)
    if away:
        base = span + SLAB
        outs[0][base : base + ROWS] = grads_ref[1, :, :PACK]
        base = base + ROWS
        for tile in range(PACK // WIDTH):
            count = min(CHUNK, ROWS - tile * CHUNK)
            column = slice(tile * WIDTH, (tile + 1) * WIDTH)
            outs[0][base : base + count, column] = grads_ref[
                1, tile * CHUNK : tile * CHUNK + count, PACK:
            ]
            if count < CHUNK:
                outs[0][base + count : base + CHUNK, column] = jnp.zeros(
                    (CHUNK - count, WIDTH), bf16
                )


def weights_pass(name, away, place, flipped, grads, sums, after):
    rows = flipped.shape[3]
    shapes = [jax.ShapeDtypeStruct((SIDE * rows + SLAB, PACK), bf16)] * SIDE
    if away:
        shapes[0] = jax.ShapeDtypeStruct((SIDE * rows + SLAB + ROWS + CHUNK, PACK), bf16)

    def whole(shape):
        return pl.BlockSpec(shape, lambda k, p: (0,) * len(shape))

    return pl.pallas_call(
        functools.partial(weights_kernel, away),
        grid_spec=pltpu.PrefetchScalarGridSpec(
            num_scalar_prefetch=1,
            grid=(1,),
            in_specs=[
                pl.BlockSpec(
                    (1,) + flipped.shape[1:],
                    lambda k, p: (1 - p[0] if away else p[0], 0, 0, 0, 0),
                ),
                whole(grads.shape),
                whole(sums.shape),
                pl.BlockSpec(memory_space=pl.ANY),
            ],
            out_specs=[whole(s.shape) for s in shapes],
        ),
        out_shape=shapes,
        compiler_params=pltpu.CompilerParams(vmem_limit_bytes=VMEM),
        cost_estimate=pl.CostEstimate(flops=10**9, bytes_accessed=4 * 10**6, transcendentals=0),
        name=name,
    )(place, flipped, grads, sums, after)


def fair_sum(terms):
    return (terms[0] + terms[3]) + (terms[1] + terms[2])


def middle_kernel(place_ref, *refs):
    inputs, outs = refs[: 2 * SIDE], refs[2 * SIDE + 1 :]
    base = place_ref[5]
    rows = outs[0].shape[1] - SLAB
    span = SIDE * rows
    for pair in range(2):
        group = inputs[pair * SIDE : (pair + 1) * SIDE]
        slab = fair_sum(
            [
                ref[span : span + SLAB, :span].astype(f32)
                + ref[span : span + SLAB, span : 2 * span].astype(f32)
                for ref in group
            ]
        )
        for k in range(SIDE):
            slot = lax.rem(base + k, SIDE)
            place = pl.ds(pl.multiple_of(slot * rows, rows), rows)
            total = group[0][place, :].astype(f32)
            for ref in group[1:]:
                total = total + ref[place, :].astype(f32)
            kind = outs[k].dtype
            outs[k][pair, :rows] = total.astype(kind)
            turned = pltpu.roll(slab, lax.rem(span - slot * rows, span), 1)[:, :WIDTH]
            high = turned.astype(bf16).astype(f32)
            outs[k][pair, rows:, :WIDTH] = high.astype(kind)
            outs[k][pair, rows:, WIDTH : 2 * WIDTH] = (turned - high).astype(bf16).astype(kind)
            outs[k][pair, rows:, 2 * WIDTH :] = jnp.zeros((SLAB, PACK - 2 * WIDTH), kind)


def total_kernel(core_ref, own_ref, one_ref, two_ref, three_ref, after_ref, *outs):
    early = core_ref[0] == 0
    rows = own_ref.shape[1] - SLAB
    sums = []
    tails = []
    refs = (own_ref, one_ref, two_ref, three_ref)
    for pair in range(2):
        total = own_ref[pair, :rows]
        for ref in refs[1:]:
            total = total + ref[pair, :rows].astype(f32)
        sums.append(total)
        slabs = [ref[pair, rows:, : 2 * WIDTH].astype(f32) for ref in refs]
        tails.append(fair_sum([t[:, :WIDTH] + t[:, WIDTH:] for t in slabs]))
    tail = tails[0] + tails[1]
    outs[3][...] = tail[: outs[3].shape[0], :rows]
    outs[4][...] = tail
    low = jnp.where(early, sums[0], sums[1])
    high = jnp.where(early, sums[1], sums[0])
    for place, out in enumerate(outs[:3]):
        cut = slice(place * PAIR, (place + 1) * PAIR)
        out[:, :PAIR] = low[:, cut]
        out[:, PAIR:] = high[:, cut]


def call(name, kernel, scalars, args, shapes, scratch=(), idle=(), flops=0, nbytes=0):
    def whole(shape):
        return pl.BlockSpec(shape, lambda i, p: (0,) * len(shape))

    return pl.pallas_call(
        kernel,
        grid_spec=pltpu.PrefetchScalarGridSpec(
            num_scalar_prefetch=1,
            grid=(1,),
            in_specs=[whole(a.shape) for a in args]
            + [pl.BlockSpec(memory_space=pl.ANY)] * len(idle),
            out_specs=[whole(s.shape) for s in shapes],
            scratch_shapes=list(scratch),
        ),
        out_shape=shapes,
        compiler_params=pltpu.CompilerParams(vmem_limit_bytes=VMEM),
        cost_estimate=pl.CostEstimate(flops=flops, bytes_accessed=nbytes, transcendentals=0),
        name=name,
    )(scalars, *args, *idle)


def input_kernel(place_ref, mine_ref, other_ref, wq_ref, wk_ref, wv_ref, wb_ref, after_ref, *outs):
    core, step = place_ref[0], pl.program_id(0)
    near = pl.ds(pl.multiple_of(core * PAIR, PAIR), PAIR)
    far = pl.ds(pl.multiple_of((1 - core) * PAIR, PAIR), PAIR)
    base = other_ref.shape[0] - CHUNK
    tiles = [
        other_ref[base : base + min(CHUNK, ROWS - t * CHUNK), t * WIDTH : (t + 1) * WIDTH]
        for t in range(PACK // WIDTH)
    ]
    shares = mine_ref[0, :, PACK:] + jnp.concatenate(tiles, 0)
    total = one(shares[:, : wb_ref.shape[0]], wb_ref[...], NN)
    base = base - ROWS
    for place, w_ref in enumerate((wq_ref, wk_ref, wv_ref)):
        cut = slice(place * PAIR, (place + 1) * PAIR)
        total = total + one(mine_ref[0, :, cut], w_ref[:, near], NT)
        total = total + one(other_ref[base : base + ROWS, cut], w_ref[:, far], NT)
    total = total.astype(bf16)
    for k, out in enumerate(outs):

        @pl.when(step == k)
        def _():
            out[...] = total


def per_device(tokens, w_query, w_key, w_value, w_beta, b_beta, d_out):
    depth = tokens.shape[1]
    index = lax.axis_index("seq")
    group = lax.axis_index("head")
    core = index % 2
    chip = index // 2
    y, x = chip % SIDE, chip // SIDE
    first, second = jnp.where(core == 0, y, x), jnp.where(core == 0, x, y)
    place = jnp.stack([core, y, x, group, first, second])
    seq = lax.axis_size("seq")
    ring = lax.axis_size("head")
    sibling = [(i, i ^ 1) for i in range(seq)]

    def swap(x):
        return lax.ppermute(x, "seq", sibling)

    other_tokens = swap(tokens)
    do_other = swap(d_out)
    wb = w_beta.T

    (projected,) = by_core(
        project_kernel,
        "project",
        place,
        [tokens, w_query, w_key, w_value, wb],
        (1, 2, 3),
        [jax.ShapeDtypeStruct((ROWS, PACK + WIDTH), f32)],
        10**9,
        5 * 10**6,
        60 * 2**20,
    )
    saved, solved, gates, own_maps, send = by_core(
        local_kernel,
        "local",
        place,
        [projected, other_tokens, w_query, w_key, w_value, wb, d_out, do_other, b_beta],
        (2, 3, 4, 6, 7),
        [
            jax.ShapeDtypeStruct((4, 3, ROWS, WIDTH), f32),
            jax.ShapeDtypeStruct((4, 4, ROWS, ROWS), bf16),
            jax.ShapeDtypeStruct((4, ROWS, WIDTH), f32),
            jax.ShapeDtypeStruct((4, 3, WIDTH, WIDTH), f32),
            jax.ShapeDtypeStruct((2, 3, WIDTH, WIDTH), STATE),
        ],
        10**10,
        10**7,
        BIG,
    )
    (extra,) = by_core(
        extra_kernel,
        "extra",
        place,
        [saved, solved, d_out, do_other],
        (2, 3),
        [jax.ShapeDtypeStruct((4, 4, ROWS, WIDTH), f32)],
        10**10,
        5 * 10**6,
        VMEM,
    )
    idle = pl.BlockSpec(memory_space=pl.ANY)

    def along(k, axis):
        route = []
        for i in range(seq):
            x, y, c = i // (2 * SIDE), i // 2 % SIDE, i % 2
            if axis(c):
                x = (x + k) % SIDE
            else:
                y = (y + k) % SIDE
            route.append((i, (x * SIDE + y) * 2 + c))
        return route

    def shift(block, k, axis):
        return lax.ppermute(block, "seq", along(k, axis))

    rows = depth // seq
    block = depth // SIDE
    layout = (2, SIDE, SIDE, rows, 2 * ROWS)
    flipped = pl.pallas_call(
        flip_kernel,
        grid=(SIDE,),
        in_specs=[pl.BlockSpec((ROWS, block), lambda i: (0, i))] * 2 + [idle],
        out_specs=pl.BlockSpec(layout, lambda i: (0,) * 5),
        out_shape=jax.ShapeDtypeStruct(layout, bf16),
        compiler_params=pltpu.CompilerParams(vmem_limit_bytes=VMEM),
        cost_estimate=pl.CostEstimate(flops=0, bytes_accessed=8 * 10**6, transcendentals=0),
        name="flip",
    )(tokens, other_tokens, send)

    far = {k: shift(send, k, lambda c: False) for k in (1, 3, 2)}
    part = (2, 2, WIDTH, WIDTH)
    span, *sends = call(
        "compose",
        compose_kernel,
        place,
        [send, far[1], far[2], far[3]],
        [jax.ShapeDtypeStruct((2, 4, WIDTH, WIDTH), f32)]
        + [jax.ShapeDtypeStruct(part, STATE)] * (SIDE - 1),
        scratch=[pltpu.VMEM((SIDE, 2, 3, WIDTH, WIDTH), STATE)],
        idle=[flipped, extra],
        flops=10**9,
    )
    far = {k: shift(sends[k - 1], k, lambda c: True) for k in (1, 3, 2)}

    grads, sums = by_core(
        back_kernel,
        "back",
        place,
        [saved, extra, gates, own_maps, d_out, do_other, span, far[1], far[2], far[3]],
        (4, 5),
        [
            jax.ShapeDtypeStruct((2, ROWS, FULL), bf16),
            jax.ShapeDtypeStruct((SLAB, WIDTH), f32),
        ],
        4 * 10**9,
        8 * 10**6,
        VMEM,
    )

    def across(k):
        return [(i, j ^ 1) for i, j in along(k, lambda c: c == 0)]

    give = weights_pass("give", 1, place, flipped, grads, sums, sums)
    given = [lax.ppermute(give[k], "seq", across(k)) for k in (0, 1, 3, 2)]
    keep = weights_pass("keep", 0, place, flipped, grads, sums, given[0])
    kept = [keep[0]] + [shift(keep[k], k, lambda c: c == 1) for k in (1, 3, 2)]

    width = depth // ring

    def full(shape):
        return pl.BlockSpec(shape, lambda i, p: (0,) * len(shape))

    def rows_at(columns):
        return pl.BlockSpec((width, columns), lambda i, p: (lax.rem(i + p[3], ring), 0))

    shifted = pl.pallas_call(
        input_kernel,
        grid_spec=pltpu.PrefetchScalarGridSpec(
            num_scalar_prefetch=1,
            grid=(ring,),
            in_specs=[full((1, ROWS, FULL)), full(given[0].shape)]
            + [rows_at(w_query.shape[1])] * 3
            + [
                pl.BlockSpec((wb.shape[0], width), lambda i, p: (0, lax.rem(i + p[3], ring))),
                idle,
            ],
            out_specs=[full((ROWS, width))] * ring,
        ),
        out_shape=[jax.ShapeDtypeStruct((ROWS, width), bf16)] * ring,
        compiler_params=pltpu.CompilerParams(vmem_limit_bytes=VMEM),
        cost_estimate=pl.CostEstimate(
            flops=4 * 10**10, bytes_accessed=8 * 10**6, transcendentals=0
        ),
        name="inputs",
    )(place, grads, given[0], w_query, w_key, w_value, wb, keep[1])

    arrived = [
        lax.ppermute(shifted[k], "head", [(i, (i + k) % ring) for i in range(ring)])
        for k in range(1, ring)
    ]
    d_x = shifted[0].astype(f32)
    for piece in arrived:
        d_x = d_x + piece.astype(f32)
    d_x = d_x.astype(bf16)

    message = (2, rows + SLAB, PACK)
    passed = call(
        "middle",
        middle_kernel,
        place,
        [*kept, *given],
        [jax.ShapeDtypeStruct(message, f32)]
        + [jax.ShapeDtypeStruct(message, bf16)] * (SIDE - 1),
        idle=[shifted[0]],
    )
    final = [shift(passed[k], k, lambda c: c == 0) for k in (1, 3, 2)]
    heads = w_beta.shape[1]
    grad_query, grad_key, grad_value, grad_wbeta, tail = call(
        "total",
        total_kernel,
        place,
        [passed[0], *final],
        [jax.ShapeDtypeStruct((rows, 2 * PAIR), f32)] * 3
        + [
            jax.ShapeDtypeStruct((heads, rows), f32),
            jax.ShapeDtypeStruct((SLAB, WIDTH), f32),
        ],
        idle=[d_x],
    )
    grad_bbeta = jnp.where(core == 0, tail, swap(tail))[4 : 4 + heads, 0]
    return (d_x, grad_query, grad_key, grad_value, grad_wbeta.T, grad_bbeta)


def solution(mesh):
    columns = P(None, "head")
    both = P("seq", "head")
    return jax.shard_map(
        per_device,
        mesh=mesh,
        in_specs=(P("seq", None), columns, columns, columns, columns, P("head"), both),
        out_specs=(both, both, both, both, both, P("head")),
        check_vma=False,
    )
```
